1024 devices in a mesh: fsdp: 32 (over y_hi, x, core), tp: 32 (over y_lo, z).
Axes of the slice: x: 4, y: 8 (y_hi: 4, y_lo: 2; y = y_hi * 2 + y_lo), z: 16, core: 2. Of those that a mesh axis runs over, the one named last changes fastest.
Arguments:
- tokens: bfloat16 [512, 12288], P('tp', 'fsdp'), may hold values from -6 to 6
- up_weight: bfloat16 [12288, 28672], P('fsdp', 'tp'), may hold values from -0.0546875 to 0.0546875
- down_weight: bfloat16 [28672, 12288], P('tp', 'fsdp'), may hold values from -0.03125 to 0.03125
- out_grad: bfloat16 [512, 12288], P('tp', 'fsdp'), may hold values from -6 to 6
Outputs:
- output: bfloat16 [512, 12288], P('tp', 'fsdp')
- in_grad: bfloat16 [512, 12288], P('tp', 'fsdp')
- up_grad: bfloat16 [12288, 28672], P('fsdp', 'tp')
- down_grad: bfloat16 [28672, 12288], P('tp', 'fsdp')
The draws below stay inside these ranges and needn't reach their ends.
All inputs are finite; a program needn't handle non-finite values.
Results may differ from the reference program's by a relative error of at most 0.0049.
Values may be sent and summed in bfloat16 or wider, within the bound.
A program may use at most 32 MiB of HBM per device.

```python
import math
import jax
import jax.numpy as jnp

D = 12288
FF = 28672
TOKENS = 512


def steps_of(stream_key, dims, cuts, low, largest):
    def one(axis_at, shards_of):
        draws = jax.random.uniform(jax.random.fold_in(jax.random.fold_in(stream_key, 6), axis_at), (shards_of,), jnp.float32, low / len(cuts), largest / len(cuts))
        return jnp.repeat(jnp.exp(draws), dims[axis_at] // shards_of).reshape((-1,) + (1,) * (len(dims) - axis_at - 1))

    loudness = one(*cuts[0])
    for cut in cuts[1:]:
        loudness = loudness * one(*cut)
    return loudness


def scatter_about(rng, shape, spread, reach, shards=(), dtype=jnp.bfloat16):
    factor_of = steps_of(rng, shape, shards, -0.22, 0.18) if shards else 1.0
    drawn = jax.random.normal(rng, shape, jnp.float32) * spread * factor_of
    return jnp.minimum(jnp.maximum(drawn, -reach), reach).astype(dtype)


def setup_inputs(seed: int = 0) -> dict:
    keys = jax.random.split(jax.random.key(seed), 5)
    return {
        "tokens": scatter_about(keys[0], (TOKENS, D), 1.0, 6.0, ((0, 32), (1, 32))),
        "up_weight": scatter_about(keys[1], (D, FF), D ** -0.5, 0.0546875, ((0, 32), (1, 32))),
        "down_weight": scatter_about(keys[2], (FF, D), FF ** -0.5, 0.03125, ((0, 32), (1, 32))),
        "out_grad": scatter_about(keys[3], (TOKENS, D), 1.0, 6.0, ((0, 32), (1, 32))),
    }


def reference(tokens, up_weight, down_weight, out_grad):
    grad_scale = 1.0 / math.sqrt(TOKENS)
    pre = jnp.dot(tokens, up_weight, preferred_element_type=jnp.float32)
    hidden = jax.nn.gelu(pre).astype(jnp.bfloat16)
    output = jnp.dot(hidden, down_weight, preferred_element_type=jnp.float32).astype(jnp.bfloat16)
    down_grad = (jnp.dot(hidden.T, out_grad, preferred_element_type=jnp.float32) * grad_scale).astype(jnp.bfloat16)
    hidden_grad = jnp.dot(out_grad, down_weight.T, preferred_element_type=jnp.float32)
    unused, pull_back = jax.vjp(jax.nn.gelu, pre)
    pre_grad = pull_back(hidden_grad)[0].astype(jnp.bfloat16)
    up_grad = (jnp.dot(tokens.T, pre_grad, preferred_element_type=jnp.float32) * grad_scale).astype(jnp.bfloat16)
    in_grad = jnp.dot(pre_grad, up_weight.T, preferred_element_type=jnp.float32).astype(jnp.bfloat16)
    return (output, in_grad, up_grad, down_grad)
```

```python
import functools
import math

import jax
import jax.numpy as jnp
from jax import lax
from jax.experimental import pallas as pl
from jax.experimental.pallas import tpu as pltpu
from jax.sharding import PartitionSpec as P

MESH = pl.DeviceIdType.MESH
BF16 = jnp.bfloat16
F32 = jnp.float32

NX, NYH, NYL, NZ = 4, 4, 2, 16
ROWS = 16
HALF = NZ * ROWS
TOKENS = NYL * HALF
FEAT, HID = 384, 896
CUT = 512
N_SEM = 288
LEAD = 6
GELU_A = math.sqrt(2.0 / math.pi)
GELU_B = 0.044715


def gelu(v):
    return 0.5 * v * (1.0 + jnp.tanh(GELU_A * (v + GELU_B * v * v * v)))


def gelu_slope(v):
    t = jnp.tanh(GELU_A * (v + GELU_B * v * v * v))
    return 0.5 * (1.0 + t) + 0.5 * v * (1.0 - t * t) * GELU_A * (1.0 + 3.0 * GELU_B * v * v)


def dot(a, b, ca=1, cb=0):
    return lax.dot_general(a, b, (((ca,), (cb,)), ((), ())), preferred_element_type=F32)


def kernel(
    tok, up, down, cot, out, in_grad, up_grad, down_grad,
    t0, t1, s0, s1, wu, wd, p0, p1, sx, rx, ry0, ry1, pre_ref, h0, h1,
    ob, rb, sum0, sum1, rz, du, dd, send_sem, recv_sem, local_sem,
):
    f = lax.axis_index("fsdp")
    t = lax.axis_index("tp")
    c = lax.rem(f, 2)
    x = lax.rem(f // 2, NX)
    yh = f // (2 * NX)
    yl = t // NZ
    z = lax.rem(t, NZ)

    def dev(x_=None, yh_=None, c_=None, yl_=None, z_=None):
        x_ = x if x_ is None else x_
        yh_ = yh if yh_ is None else yh_
        c_ = c if c_ is None else c_
        yl_ = yl if yl_ is None else yl_
        z_ = z if z_ is None else z_
        return ((yh_ * NX + x_) * 2 + c_, yl_ * NZ + z_)

    def mod(v, n):
        return lax.rem(v + n, n)

    xp, xm, xo = mod(x + 1, NX), mod(x - 1, NX), mod(x + 2, NX)
    yp, ym, yo = mod(yh + 1, NYH), mod(yh - 1, NYH), mod(yh + 2, NYH)
    sibling, partner = dev(c_=1 - c), dev(yl_=1 - yl)
    x_up, x_down = dev(x_=xp), dev(x_=xm)
    y_up, y_down = dev(yh_=yp), dev(yh_=ym)
    z_up, z_down = dev(z_=mod(z + 1, NZ)), dev(z_=mod(z - 1, NZ))

    pending = []
    used = [0, 0]

    def local(src, dst):
        copy = pltpu.make_async_copy(src, dst, local_sem.at[used[1]])
        used[1] += 1
        copy.start()
        return copy

    def send(src, dst, to):
        copy = pltpu.make_async_remote_copy(
            src_ref=src, dst_ref=dst, send_sem=send_sem.at[used[0]], recv_sem=recv_sem.at[used[0]],
            device_id=to, device_id_type=MESH,
        )
        used[0] += 1
        copy.start()
        pending.append(copy)
        return copy

    def zrows(k):
        return pl.ds(pl.multiple_of(mod(z + k, NZ) * ROWS, ROWS), ROWS)

    weights = [local(up, wu.at[0]), local(down, wd.at[0])]
    own_rows = [
        local(src, buf.at[yl, zrows(0), :]) for src, buf in ((tok, t0), (cot, t1))
    ]

    barrier = pltpu.get_barrier_semaphore()
    peers = (sibling, partner, x_up, x_down, y_up, y_down, z_up, z_down)
    for peer in peers:
        pl.semaphore_signal(barrier, inc=1, device_id=peer, device_id_type=MESH)
    pl.semaphore_wait(barrier, len(peers))

    done = set()
    weight_copies = []

    def chain(a):
        src, rows_all, rows_sib, part, h, total, result = (
            (tok, t0, s0, p0, h0, sum0, out), (cot, t1, s1, p1, h1, sum1, in_grad)
        )[a]
        long, short = ((z_up, z_down), (z_down, z_up))[a]
        sign = (1, -1)[a]

        first = send(src, rows_all.at[yl, zrows(0), :], partner)
        yield
        forwards = []

        def forward(k):
            forwards.append(send(rows_all.at[1 - c, zrows(k), :], rows_sib.at[zrows(k), :], sibling))

        own_rows[a].wait()
        first.wait_recv()
        to_forward = [0]
        for hop in range(NZ // 2):
            k = -sign * hop
            one = send(rows_all.at[:, zrows(k), :], rows_all.at[:, zrows(k), :], long)
            two = None
            if hop < NZ // 2 - 1:
                two = send(rows_all.at[:, zrows(-k), :], rows_all.at[:, zrows(-k), :], short)
            for k_ in to_forward:
                forward(k_)
            if a == 0 and hop == 0:
                weight_copies.extend((send(up, wu.at[1], sibling), send(down, wd.at[1], sibling)))
            yield
            one.wait_recv()
            to_forward = [k - sign]
            if two is not None:
                two.wait_recv()
                to_forward.append(-k + sign)
        for k_ in to_forward:
            forward(k_)
        done.add(("rows", a))
        yield
        for copy in forwards:
            copy.wait_recv()

        if a == 0:
            weights[0].wait()
            weight_copies[0].wait_recv()
            part[...] = dot(rows_all[c], wu[0]) + dot(rows_sib[...], wu[1])
        else:
            weights[1].wait()
            weight_copies[1].wait_recv()
            part[...] = dot(rows_all[c], wd[0], 1, 1) + dot(rows_sib[...], wd[1], 1, 1)

        def xrows(x_, half):
            return pl.ds(pl.multiple_of(x_ * 64 + half * 32, 32), 32)

        def put(k, x_, half, to, add=None):
            value = part[xrows(x_, half), :]
            if add is not None:
                value = value + rx[a, add].astype(F32)
            sx[a, k] = value.astype(BF16)
            return send(sx.at[a, k], rx.at[a, k], to)

        m0 = put(0, xo, 0, x_up)
        m1 = put(1, xo, 1, x_down)
        m2 = put(2, xp, 1, x_up)
        m3 = put(3, xm, 0, x_down)
        yield
        m0.wait_recv()
        m4 = put(4, xp, 0, x_up, 0)
        m1.wait_recv()
        m5 = put(5, xm, 1, x_down, 1)
        yield
        m3.wait_recv()
        m2.wait_recv()
        m4.wait_recv()
        part[xrows(x, 0), :] += rx[a, 3].astype(F32) + rx[a, 4].astype(F32)
        m5.wait_recv()
        part[xrows(x, 1), :] += rx[a, 2].astype(F32) + rx[a, 5].astype(F32)

        def yrows(y_):
            return pl.ds(pl.multiple_of(x * 64 + y_ * ROWS, ROWS), ROWS)

        lo, hi = pl.ds(0, CUT), pl.ds(CUT, HID - CUT)
        n0 = send(part.at[yrows(yo), lo], ry0.at[a, 0], y_up)
        n1 = send(part.at[yrows(yo), hi], ry1.at[a, 0], y_down)
        n2 = send(part.at[yrows(yp), hi], ry1.at[a, 1], y_up)
        n3 = send(part.at[yrows(ym), lo], ry0.at[a, 1], y_down)
        yield
        n0.wait_recv()
        part[yrows(yp), lo] += ry0[a, 0]
        n4 = send(part.at[yrows(yp), lo], ry0.at[a, 2], y_up)
        n1.wait_recv()
        part[yrows(ym), hi] += ry1[a, 0]
        n5 = send(part.at[yrows(ym), hi], ry1.at[a, 2], y_down)
        yield
        n2.wait_recv()
        n3.wait_recv()
        n4.wait_recv()
        n5.wait_recv()
        part[yrows(yh), lo] += ry0[a, 1] + ry0[a, 2]
        part[yrows(yh), hi] += ry1[a, 1] + ry1[a, 2]

        def hrows(x_, y_):
            return pl.ds(pl.multiple_of(c * HALF + x_ * 64 + y_ * ROWS, ROWS), ROWS)

        value = part[yrows(yh), :]
        if a == 0:
            pre_ref[...] = value
            h[hrows(x, yh), :] = gelu(value).astype(BF16)
            done.add("pre")
        else:
            assert "pre" in done
            h[hrows(x, yh), :] = (value * gelu_slope(pre_ref[...])).astype(BF16)

        def block(x_, y_, to, cols=None):
            ref = h.at[hrows(x_, y_), :] if cols is None else h.at[hrows(x_, y_), cols]
            return send(ref, ref, to)

        def column(x_):
            rows = pl.ds(pl.multiple_of(c * HALF + x_ * 64, 64), 64)
            return send(h.at[rows, :], h.at[rows, :], sibling)

        ya, yb = block(x, yh, y_up), block(x, yh, y_down)
        xa0, xb0 = block(x, yh, x_up), block(x, yh, x_down)
        yield
        ya.wait_recv()
        yc = block(x, ym, y_up, lo)
        xa1, xb1 = block(x, ym, x_up), block(x, ym, x_down)
        yb.wait_recv()
        yd = block(x, yp, y_down, hi)
        xa2, xb2 = block(x, yp, x_up), block(x, yp, x_down)
        yield
        xa0.wait_recv()
        relays = [block(xm, yh, x_up)]
        yc.wait_recv()
        yd.wait_recv()
        xa3, xb3 = block(x, yo, x_up), block(x, yo, x_down)
        columns = [column(x)]
        yield
        xa1.wait_recv()
        relays.append(block(xm, ym, x_up))
        xb2.wait_recv()
        relays.append(block(xp, yp, x_down))
        yield
        xb3.wait_recv()
        relays.append(block(xp, yo, x_down))
        xb0.wait_recv()
        xb1.wait_recv()
        columns.append(column(xp))
        xa2.wait_recv()
        xa3.wait_recv()
        columns.append(column(xm))
        yield
        for copy in relays:
            copy.wait_recv()
        columns.append(column(xo))
        yield
        for copy in columns:
            copy.wait_recv()
        done.add(("hidden", a))

        def product(half):
            rows = h[pl.ds(pl.multiple_of(half * HALF, HALF), HALF), :]
            return dot(rows, wd[0]) if a == 0 else dot(rows, wu[0], 1, 1)

        ob[a] = product(1 - yl).astype(BF16)
        order = [sign * (NZ // 2)]
        for k in range(NZ // 2 - 1, 0, -1):
            order += [sign * k, -sign * k]
        order.append(0)
        across = {}
        for k in order:
            across[k] = send(ob.at[a, zrows(k), :], rb.at[a, zrows(k), :], partner)
        total[...] = product(yl)

        one = two = None
        for hop in range(NZ // 2):
            yield
            k = sign * (NZ // 2 - hop)
            across[k].wait_recv()
            value = total[zrows(k), :] + rb[a, zrows(k), :].astype(F32)
            if one is not None:
                one.wait_recv()
                value = value + rz[a, hop - 1]
            total[zrows(k), :] = value
            one = send(total.at[zrows(k), :], rz.at[a, hop], long)
            if hop >= 1:
                across[-k].wait_recv()
                value = total[zrows(-k), :] + rb[a, zrows(-k), :].astype(F32)
                if two is not None:
                    two.wait_recv()
                    value = value + rz[a, NZ // 2 + hop - 2]
                total[zrows(-k), :] = value
                two = send(total.at[zrows(-k), :], rz.at[a, NZ // 2 + hop - 1], short)
        yield
        across[0].wait_recv()
        value = total[zrows(0), :] + rb[a, zrows(0), :].astype(F32)
        one.wait_recv()
        two.wait_recv()
        value = value + (rz[a, NZ // 2 - 1] + rz[a, NZ - 2])
        result[...] = value.astype(BF16)

    scale = 1.0 / math.sqrt(TOKENS)
    grads = []

    def down_product():
        dd[...] = (dot(h0[...], t1[...].reshape(TOKENS, FEAT), 0, 0) * scale).astype(BF16)
        grads.append(local(dd, down_grad))

    def up_product():
        du[...] = (dot(t0[...].reshape(TOKENS, FEAT), h1[...], 0, 0) * scale).astype(BF16)
        grads.append(local(du, up_grad))

    forward_chain, backward_chain = chain(0), chain(1)
    live = [True, True]
    todo = [down_product, up_product]

    def advance(which, gen):
        if live[which] and next(gen, "end") == "end":
            live[which] = False

    step = 0
    while any(live):
        advance(0, forward_chain)
        if step >= LEAD:
            advance(1, backward_chain)
        step += 1
        for index, need in ((0, (("hidden", 0), ("rows", 1))), (1, (("hidden", 1),))):
            if todo[index] is not None and all(n in done for n in need):
                todo[index]()
                todo[index] = None
                break

    assert all(job is None for job in todo)
    for copy in pending:
        copy.wait_send()
    for copy in grads:
        copy.wait()


def body(tokens, up_weight, down_weight, out_grad):
    anywhere = pl.BlockSpec(memory_space=pl.ANY)
    vmem = pl.BlockSpec(memory_space=pltpu.VMEM)
    return pl.pallas_call(
        kernel,
        out_shape=(
            jax.ShapeDtypeStruct((ROWS, FEAT), BF16),
            jax.ShapeDtypeStruct((ROWS, FEAT), BF16),
            jax.ShapeDtypeStruct((FEAT, HID), BF16),
            jax.ShapeDtypeStruct((HID, FEAT), BF16),
        ),
        in_specs=[anywhere] * 4,
        out_specs=(vmem, vmem, anywhere, anywhere),
        scratch_shapes=[
            pltpu.VMEM((NYL, HALF, FEAT), BF16),
            pltpu.VMEM((NYL, HALF, FEAT), BF16),
            pltpu.VMEM((HALF, FEAT), BF16),
            pltpu.VMEM((HALF, FEAT), BF16),
            pltpu.VMEM((2, FEAT, HID), BF16),
            pltpu.VMEM((2, HID, FEAT), BF16),
            pltpu.VMEM((HALF, HID), F32),
            pltpu.VMEM((HALF, HID), F32),
            pltpu.VMEM((2, 6, 32, HID), BF16),
            pltpu.VMEM((2, 6, 32, HID), BF16),
            pltpu.VMEM((2, 3, ROWS, CUT), F32),
            pltpu.VMEM((2, 3, ROWS, HID - CUT), F32),
            pltpu.VMEM((ROWS, HID), F32),
            pltpu.VMEM((TOKENS, HID), BF16),
            pltpu.VMEM((TOKENS, HID), BF16),
            pltpu.VMEM((2, HALF, FEAT), BF16),
            pltpu.VMEM((2, HALF, FEAT), BF16),
            pltpu.VMEM((HALF, FEAT), F32),
            pltpu.VMEM((HALF, FEAT), F32),
            pltpu.VMEM((2, NZ - 1, ROWS, FEAT), F32),
            pltpu.VMEM((FEAT, HID), BF16),
            pltpu.VMEM((HID, FEAT), BF16),
            pltpu.SemaphoreType.DMA((N_SEM,)),
            pltpu.SemaphoreType.DMA((N_SEM,)),
            pltpu.SemaphoreType.DMA((8,)),
        ],
        compiler_params=pltpu.CompilerParams(
            collective_id=0, has_side_effects=True, vmem_limit_bytes=48 * 1024 * 1024
        ),
    )(tokens, up_weight, down_weight, out_grad)


def solution(mesh):
    return jax.shard_map(
        body,
        mesh=mesh,
        in_specs=(P("tp", "fsdp"), P("fsdp", "tp"), P("tp", "fsdp"), P("tp", "fsdp")),
        out_specs=(P("tp", "fsdp"), P("tp", "fsdp"), P("fsdp", "tp"), P("tp", "fsdp")),
        check_vma=False,
    )
```

```python
import functools
import math

import jax
import jax.numpy as jnp
from jax import lax
from jax.experimental import pallas as pl
from jax.experimental.pallas import tpu as pltpu
from jax.sharding import PartitionSpec as P

MESH = pl.DeviceIdType.MESH
BF16 = jnp.bfloat16
F32 = jnp.float32

NX, NYH, NYL, NZ = 4, 4, 2, 16
ROWS = 16
HALF = NZ * ROWS
TOKENS = NYL * HALF
FEAT, HID = 384, 896
AWAY = (2, 1, -1)
Z_AWAY = (8,) + tuple(s * k for k in range(7, 0, -1) for s in (1, -1))
N_SEM = 176
ORDER = "FBFFBFBFBFBFBFBFBGBGFB"
GELU_A = math.sqrt(2.0 / math.pi)
GELU_B = 0.044715


def gelu(v):
    return 0.5 * v * (1.0 + jnp.tanh(GELU_A * (v + GELU_B * v * v * v)))


def gelu_slope(v):
    t = jnp.tanh(GELU_A * (v + GELU_B * v * v * v))
    return 0.5 * (1.0 + t) + 0.5 * v * (1.0 - t * t) * GELU_A * (1.0 + 3.0 * GELU_B * v * v)


def dot(a, b, ca=1, cb=0):
    return lax.dot_general(a, b, (((ca,), (cb,)), ((), ())), preferred_element_type=F32)


def kernel(
    tok, up, down, cot, out, in_grad, up_grad, down_grad,
    t0, t1, s0, s1, wu, wd, p0, p1, sx, rx, ry, pre_ref, h0, h1,
    ob, rb, sum0, sum1, zs, rz, du, dd, send_sem, recv_sem, local_sem,
):
    f = lax.axis_index("fsdp")
    t = lax.axis_index("tp")
    c = lax.rem(f, 2)
    x = lax.rem(f // 2, NX)
    yh = f // (2 * NX)
    yl = t // NZ
    z = lax.rem(t, NZ)

    def dev(x_=None, yh_=None, c_=None, yl_=None, z_=None):
        x_ = x if x_ is None else x_
        yh_ = yh if yh_ is None else yh_
        c_ = c if c_ is None else c_
        yl_ = yl if yl_ is None else yl_
        z_ = z if z_ is None else z_
        return ((yh_ * NX + x_) * 2 + c_, yl_ * NZ + z_)

    def mod(v, n):
        return lax.rem(v + n, n)

    sibling, partner = dev(c_=1 - c), dev(yl_=1 - yl)
    x_peers = [mod(x + k, NX) for k in AWAY]
    y_peers = [mod(yh + k, NYH) for k in AWAY]
    x_devs = [dev(x_=v) for v in x_peers]
    y_devs = [dev(yh_=v) for v in y_peers]
    z_devs = [dev(z_=mod(z + k, NZ)) for k in Z_AWAY]

    pending = []
    used = [0, 0]

    def local(src, dst):
        copy = pltpu.make_async_copy(src, dst, local_sem.at[used[1]])
        used[1] += 1
        copy.start()
        return copy

    def send(src, dst, to):
        copy = pltpu.make_async_remote_copy(
            src_ref=src, dst_ref=dst, send_sem=send_sem.at[used[0]], recv_sem=recv_sem.at[used[0]],
            device_id=to, device_id_type=MESH,
        )
        used[0] += 1
        copy.start()
        pending.append(copy)
        return copy

    def zrows(k):
        return pl.ds(pl.multiple_of(mod(z + k, NZ) * ROWS, ROWS), ROWS)

    weights = [local(up, wu.at[0]), local(down, wd.at[0])]
    own_rows = [
        local(src, buf.at[yl, zrows(0), :]) for src, buf in ((tok, t0), (cot, t1))
    ]

    barrier = pltpu.get_barrier_semaphore()
    peers = (sibling, partner, *x_devs, *y_devs, *z_devs)
    for peer in peers:
        pl.semaphore_signal(barrier, inc=1, device_id=peer, device_id_type=MESH)
    pl.semaphore_wait(barrier, len(peers))

    done = set()
    weight_copies = []

    def chain(a):
        src, rows_all, rows_sib, part, h, total, result = (
            (tok, t0, s0, p0, h0, sum0, out), (cot, t1, s1, p1, h1, sum1, in_grad)
        )[a]

        mine = rows_all.at[yl, zrows(0), :]
        over_z = [send(src, mine, to) for to in z_devs]
        over_y = [send(src, mine, partner)]
        if a == 0:
            weight_copies.extend((send(up, wu.at[1], sibling), send(down, wd.at[1], sibling)))
        yield
        own_rows[a].wait()
        for k, copy in reversed(tuple(zip(Z_AWAY, over_z))):
            copy.wait_recv()
            there = rows_all.at[yl, zrows(-k), :]
            over_y.append(send(there, there, partner))
        yield
        for copy in over_y:
            copy.wait_recv()
        across = send(rows_all.at[1 - c], rows_sib, sibling)
        done.add(("rows", a))

        w, contract = ((wu, 0), (wd, 1))[a]
        weights[a].wait()
        part[...] = dot(rows_all[c], w[0], 1, contract)
        weight_copies[a].wait_recv()
        across.wait_recv()
        part[...] += dot(rows_sib[...], w[1], 1, contract)

        def xrows(x_):
            return pl.ds(pl.multiple_of(x_ * 64, 64), 64)

        copies = []
        for i, (there, to) in enumerate(zip(x_peers, x_devs)):
            sx[a, i] = part[xrows(there), :].astype(BF16)
            copies.append(send(sx.at[a, i], rx.at[a, i], to))
        yield
        for copy in copies:
            copy.wait_recv()
        part[xrows(x), :] += rx[a, 0].astype(F32) + rx[a, 1].astype(F32) + rx[a, 2].astype(F32)

        def yrows(y_):
            return pl.ds(pl.multiple_of(x * 64 + y_ * ROWS, ROWS), ROWS)

        copies = [
            send(part.at[yrows(there), :], ry.at[a, i], to)
            for i, (there, to) in enumerate(zip(y_peers, y_devs))
        ]
        yield
        for copy in copies:
            copy.wait_recv()
        value = part[yrows(yh), :] + (ry[a, 0] + ry[a, 1] + ry[a, 2])

        def hrows(x_, y_):
            return pl.ds(pl.multiple_of(c * HALF + x_ * 64 + y_ * ROWS, ROWS), ROWS)

        if a == 0:
            pre_ref[...] = value
            h[hrows(x, yh), :] = gelu(value).astype(BF16)
            done.add("pre")
        else:
            assert "pre" in done
            h[hrows(x, yh), :] = (value * gelu_slope(pre_ref[...])).astype(BF16)

        def block(y_, to):
            ref = h.at[hrows(x, y_), :]
            return send(ref, ref, to)

        def column(x_):
            rows = pl.ds(pl.multiple_of(c * HALF + x_ * 64, 64), 64)
            return send(h.at[rows, :], h.at[rows, :], sibling)

        over_yh = [block(yh, to) for to in y_devs]
        over_x = [[block(yh, to)] for to in x_devs]
        yield
        for i in (1, 2, 0):
            over_yh[i].wait_recv()
            for copies, to in zip(over_x, x_devs):
                copies.append(block(mod(yh - AWAY[i], NYH), to))
        columns = [column(x)]
        yield
        for i in (1, 2, 0):
            for copy in over_x[i]:
                copy.wait_recv()
            columns.append(column(mod(x - AWAY[i], NX)))
        yield
        for copy in columns:
            copy.wait_recv()
        done.add(("hidden", a))

        back, contract = ((wd, 0), (wu, 1))[a]

        def product(first, n):
            rows = h[pl.ds(pl.multiple_of(first, 128), n), :]
            return dot(rows, back[0], 1, contract)

        copies = []
        for i in range(2):
            rows = pl.ds(i * 128, 128)
            ob[a, rows, :] = product((1 - yl) * HALF + i * 128, 128).astype(BF16)
            copies.append(send(ob.at[a, rows, :], rb.at[a, rows, :], partner))
        total[...] = product(yl * HALF, HALF)
        yield
        for i, copy in enumerate(copies):
            rows = pl.ds(i * 128, 128)
            copy.wait_recv()
            total[rows, :] += rb[a, rows, :].astype(F32)

        zs[a] = total[...].astype(BF16)
        copies = [
            send(zs.at[a, zrows(k), :], rz.at[a, i], to)
            for i, (k, to) in enumerate(zip(Z_AWAY, z_devs))
        ]
        yield
        value = total[zrows(0), :]
        for i, copy in reversed(tuple(enumerate(copies))):
            copy.wait_recv()
            value = value + rz[a, i].astype(F32)
        result[...] = value.astype(BF16)

    scale = 1.0 / math.sqrt(TOKENS)
    grads = []

    def down_product():
        dd[...] = (dot(h0[...], t1[...].reshape(TOKENS, FEAT), 0, 0) * scale).astype(BF16)
        grads.append(local(dd, down_grad))

    def up_product():
        du[...] = (dot(t0[...].reshape(TOKENS, FEAT), h1[...], 0, 0) * scale).astype(BF16)
        grads.append(local(du, up_grad))

    steps = {
        "F": chain(0), "B": chain(1), "G": iter((down_product, up_product)),
    }
    for name in ORDER:
        step = next(steps[name], None)
        if step is not None:
            step()
    assert next(steps["F"], "end") == next(steps["B"], "end") == next(steps["G"], "end") == "end"

    for copy in pending:
        copy.wait_send()
    for copy in grads:
        copy.wait()


def body(tokens, up_weight, down_weight, out_grad):
    anywhere = pl.BlockSpec(memory_space=pl.ANY)
    vmem = pl.BlockSpec(memory_space=pltpu.VMEM)
    return pl.pallas_call(
        kernel,
        out_shape=(
            jax.ShapeDtypeStruct((ROWS, FEAT), BF16),
            jax.ShapeDtypeStruct((ROWS, FEAT), BF16),
            jax.ShapeDtypeStruct((FEAT, HID), BF16),
            jax.ShapeDtypeStruct((HID, FEAT), BF16),
        ),
        in_specs=[anywhere] * 4,
        out_specs=(vmem, vmem, anywhere, anywhere),
        scratch_shapes=[
            pltpu.VMEM((NYL, HALF, FEAT), BF16),
            pltpu.VMEM((NYL, HALF, FEAT), BF16),
            pltpu.VMEM((HALF, FEAT), BF16),
            pltpu.VMEM((HALF, FEAT), BF16),
            pltpu.VMEM((2, FEAT, HID), BF16),
            pltpu.VMEM((2, HID, FEAT), BF16),
            pltpu.VMEM((HALF, HID), F32),
            pltpu.VMEM((HALF, HID), F32),
            pltpu.VMEM((2, 3, 64, HID), BF16),
            pltpu.VMEM((2, 3, 64, HID), BF16),
            pltpu.VMEM((2, 3, ROWS, HID), F32),
            pltpu.VMEM((ROWS, HID), F32),
            pltpu.VMEM((TOKENS, HID), BF16),
            pltpu.VMEM((TOKENS, HID), BF16),
            pltpu.VMEM((2, HALF, FEAT), BF16),
            pltpu.VMEM((2, HALF, FEAT), BF16),
            pltpu.VMEM((HALF, FEAT), F32),
            pltpu.VMEM((HALF, FEAT), F32),
            pltpu.VMEM((2, HALF, FEAT), BF16),
            pltpu.VMEM((2, NZ - 1, ROWS, FEAT), BF16),
            pltpu.VMEM((FEAT, HID), BF16),
            pltpu.VMEM((HID, FEAT), BF16),
            pltpu.SemaphoreType.DMA((N_SEM,)),
            pltpu.SemaphoreType.DMA((N_SEM,)),
            pltpu.SemaphoreType.DMA((8,)),
        ],
        compiler_params=pltpu.CompilerParams(
            collective_id=0, has_side_effects=True, vmem_limit_bytes=60 * 1024 * 1024
        ),
    )(tokens, up_weight, down_weight, out_grad)


def solution(mesh):
    return jax.shard_map(
        body,
        mesh=mesh,
        in_specs=(P("tp", "fsdp"), P("fsdp", "tp"), P("tp", "fsdp"), P("tp", "fsdp")),
        out_specs=(P("tp", "fsdp"), P("tp", "fsdp"), P("fsdp", "tp"), P("tp", "fsdp")),
        check_vma=False,
    )
```

```python
import functools
import math

import jax
import jax.numpy as jnp
from jax import lax
from jax.experimental import pallas as pl
from jax.experimental.pallas import tpu as pltpu
from jax.sharding import PartitionSpec as P

MESH = pl.DeviceIdType.MESH
BF16 = jnp.bfloat16
F32 = jnp.float32

NX, NYH, NYL, NZ = 4, 4, 2, 16
ROWS = 16
HALF = NZ * ROWS
TOKENS = NYL * HALF
FEAT, HID = 384, 896
AWAY = (2, 1, -1)
Z_AWAY = (8,) + tuple(s * k for k in range(7, 0, -1) for s in (1, -1))
Z_DIRECT = (8, 6, -6, 3, -3, 1, -1)
N_SEM = 208
ORDER = "FBFBFFBFBFBFBFFBFBBGBGFB"
GELU_A = math.sqrt(2.0 / math.pi)
GELU_B = 0.044715


def gelu(v):
    return 0.5 * v * (1.0 + jnp.tanh(GELU_A * (v + GELU_B * v * v * v)))


def gelu_slope(v):
    t = jnp.tanh(GELU_A * (v + GELU_B * v * v * v))
    return 0.5 * (1.0 + t) + 0.5 * v * (1.0 - t * t) * GELU_A * (1.0 + 3.0 * GELU_B * v * v)


def dot(a, b, ca=1, cb=0):
    return lax.dot_general(a, b, (((ca,), (cb,)), ((), ())), preferred_element_type=F32)


def kernel(
    tok, up, down, cot, out, in_grad, up_grad, down_grad,
    t0, t1, s0, s1, wu, wd, p0, p1, sx, rx, sy0, sy1, ry0, ry1, pre_ref, h0, h1,
    ob, rb, sum0, sum1, zs, rz, du, dd, send_sem, recv_sem, local_sem,
):
    f = lax.axis_index("fsdp")
    t = lax.axis_index("tp")
    c = lax.rem(f, 2)
    x = lax.rem(f // 2, NX)
    yh = f // (2 * NX)
    yl = t // NZ
    z = lax.rem(t, NZ)

    def dev(x_=None, yh_=None, c_=None, yl_=None, z_=None):
        x_ = x if x_ is None else x_
        yh_ = yh if yh_ is None else yh_
        c_ = c if c_ is None else c_
        yl_ = yl if yl_ is None else yl_
        z_ = z if z_ is None else z_
        return ((yh_ * NX + x_) * 2 + c_, yl_ * NZ + z_)

    def mod(v, n):
        return lax.rem(v + n, n)

    sibling, partner = dev(c_=1 - c), dev(yl_=1 - yl)
    x_peers = [mod(x + k, NX) for k in AWAY]
    y_peers = [mod(yh + k, NYH) for k in AWAY]
    x_devs = [dev(x_=v) for v in x_peers]
    y_devs = [dev(yh_=v) for v in y_peers]

    def z_dev(k):
        return dev(z_=mod(z + k, NZ))

    z_devs = [z_dev(k) for k in Z_AWAY]

    pending = []
    used = [0, 0]

    def local(src, dst):
        copy = pltpu.make_async_copy(src, dst, local_sem.at[used[1]])
        used[1] += 1
        copy.start()
        return copy

    def send(src, dst, to):
        copy = pltpu.make_async_remote_copy(
            src_ref=src, dst_ref=dst, send_sem=send_sem.at[used[0]], recv_sem=recv_sem.at[used[0]],
            device_id=to, device_id_type=MESH,
        )
        used[0] += 1
        copy.start()
        pending.append(copy)
        return copy

    def zrows(k):
        return pl.ds(pl.multiple_of(mod(z + k, NZ) * ROWS, ROWS), ROWS)

    weights = [local(up, wu.at[0]), local(down, wd.at[0])]
    own_rows = [
        local(src, buf.at[yl, zrows(0), :]) for src, buf in ((tok, t0), (cot, t1))
    ]

    barrier = pltpu.get_barrier_semaphore()
    peers = (sibling, partner, *x_devs, *y_devs, *z_devs)
    for peer in peers:
        pl.semaphore_signal(barrier, inc=1, device_id=peer, device_id_type=MESH)
    pl.semaphore_wait(barrier, len(peers))

    done = set()
    weight_copies = []

    def chain(a):
        src, rows_all, rows_sib, part, h, total, result = (
            (tok, t0, s0, p0, h0, sum0, out), (cot, t1, s1, p1, h1, sum1, in_grad)
        )[a]

        mine = rows_all.at[yl, zrows(0), :]
        direct = {k: send(src, mine, z_dev(k)) for k in Z_DIRECT}
        over_y = [send(src, mine, partner)]
        if a == 0:
            weight_copies.extend((send(up, wu.at[1], sibling), send(down, wd.at[1], sibling)))
        yield

        def cross(k):
            there = rows_all.at[yl, zrows(-k), :]
            over_y.append(send(there, there, partner))

        passed = {}
        for k in (1, -1, 3, -3, 6, -6):
            direct[k].wait_recv()
            if abs(k) > 1:
                there = rows_all.at[yl, zrows(-k), :]
                for s in (1, -1):
                    passed[k + s] = send(there, there, z_dev(s))
            cross(k)
        yield
        direct[8].wait_recv()
        cross(8)
        for k, copy in passed.items():
            copy.wait_recv()
            cross(k)
        own_rows[a].wait()
        yield
        for copy in over_y:
            copy.wait_recv()
        across = send(rows_all.at[1 - c], rows_sib, sibling)
        done.add(("rows", a))

        w, contract = ((wu, 0), (wd, 1))[a]
        weights[a].wait()
        part[...] = dot(rows_all[c], w[0], 1, contract)
        weight_copies[a].wait_recv()
        across.wait_recv()
        part[...] += dot(rows_sib[...], w[1], 1, contract)

        def xrows(x_):
            return pl.ds(pl.multiple_of(x_ * 64, 64), 64)

        for i, there in enumerate(x_peers):
            sx[a, i] = part[xrows(there), :].astype(BF16)
        over_x = []
        for there in y_peers + [yh]:
            rows = pl.ds(pl.multiple_of(there * ROWS, ROWS), ROWS)
            over_x.append(
                [send(sx.at[a, i, rows, :], rx.at[a, i, rows, :], to) for i, to in enumerate(x_devs)]
            )
        yield

        def yrows(y_):
            return pl.ds(pl.multiple_of(x * 64 + y_ * ROWS, ROWS), ROWS)

        def sum_x(j, there):
            for copy in over_x[j]:
                copy.wait_recv()
            rows = pl.ds(pl.multiple_of(there * ROWS, ROWS), ROWS)
            got = rx[a, :, rows, :].astype(F32)
            return part[yrows(there), :] + (got[0] + got[1] + got[2])

        copies = []
        for i, (there, to) in enumerate(zip(y_peers, y_devs)):
            value = sum_x(i, there)
            if a == 0:
                sy0[i] = value.astype(BF16)
                copies.append(send(sy0.at[i], ry0.at[i], to))
            else:
                sy1[i] = value
                copies.append(send(sy1.at[i], ry1.at[i], to))
        yield
        value = sum_x(3, yh)
        for copy in copies:
            copy.wait_recv()
        got = ry0[...].astype(F32) if a == 0 else ry1[...]
        value = value + (got[0] + got[1] + got[2])

        def hrows(x_, y_):
            return pl.ds(pl.multiple_of(c * HALF + x_ * 64 + y_ * ROWS, ROWS), ROWS)

        if a == 0:
            pre_ref[...] = value
            h[hrows(x, yh), :] = gelu(value).astype(BF16)
            done.add("pre")
        else:
            assert "pre" in done
            h[hrows(x, yh), :] = (value * gelu_slope(pre_ref[...])).astype(BF16)

        def block(y_, to):
            ref = h.at[hrows(x, y_), :]
            return send(ref, ref, to)

        def column(x_):
            rows = pl.ds(pl.multiple_of(c * HALF + x_ * 64, 64), 64)
            return send(h.at[rows, :], h.at[rows, :], sibling)

        over_yh = [block(yh, to) for to in y_devs]
        over_x = [[block(yh, to)] for to in x_devs]
        yield
        for i in (1, 2, 0):
            over_yh[i].wait_recv()
            for copies, to in zip(over_x, x_devs):
                copies.append(block(mod(yh - AWAY[i], NYH), to))
        columns = [column(x)]
        yield
        for i in (1, 2, 0):
            for copy in over_x[i]:
                copy.wait_recv()
            columns.append(column(mod(x - AWAY[i], NX)))
        yield
        for copy in columns:
            copy.wait_recv()
        done.add(("hidden", a))

        back, contract = ((wd, 0), (wu, 1))[a]

        def product(half):
            rows = h[pl.ds(pl.multiple_of(half * HALF, HALF), HALF), :]
            return dot(rows, back[0], 1, contract)

        ob[a] = product(1 - yl).astype(BF16)
        across = [
            send(ob.at[a, zrows(k), :], rb.at[a, zrows(k), :], partner) for k in Z_AWAY + (0,)
        ]
        total[...] = product(yl)
        yield

        copies = []
        for i, (k, to) in enumerate(zip(Z_AWAY, z_devs)):
            across[i].wait_recv()
            zs[a, zrows(k), :] = (total[zrows(k), :] + rb[a, zrows(k), :].astype(F32)).astype(BF16)
            copies.append(send(zs.at[a, zrows(k), :], rz.at[a, i], to))
        across[-1].wait_recv()
        yield
        value = total[zrows(0), :] + rb[a, zrows(0), :].astype(F32)
        for i, copy in reversed(tuple(enumerate(copies))):
            copy.wait_recv()
            value = value + rz[a, i].astype(F32)
        result[...] = value.astype(BF16)

    scale = 1.0 / math.sqrt(TOKENS)
    grads = []

    def down_product():
        dd[...] = (dot(h0[...], t1[...].reshape(TOKENS, FEAT), 0, 0) * scale).astype(BF16)
        grads.append(local(dd, down_grad))

    def up_product():
        du[...] = (dot(t0[...].reshape(TOKENS, FEAT), h1[...], 0, 0) * scale).astype(BF16)
        grads.append(local(du, up_grad))

    steps = {
        "F": chain(0), "B": chain(1), "G": iter((down_product, up_product)),
    }
    for name in ORDER:
        step = next(steps[name], None)
        if step is not None:
            step()
    assert next(steps["F"], "end") == next(steps["B"], "end") == next(steps["G"], "end") == "end"

    for copy in pending:
        copy.wait_send()
    for copy in grads:
        copy.wait()


def body(tokens, up_weight, down_weight, out_grad):
    anywhere = pl.BlockSpec(memory_space=pl.ANY)
    vmem = pl.BlockSpec(memory_space=pltpu.VMEM)
    return pl.pallas_call(
        kernel,
        out_shape=(
            jax.ShapeDtypeStruct((ROWS, FEAT), BF16),
            jax.ShapeDtypeStruct((ROWS, FEAT), BF16),
            jax.ShapeDtypeStruct((FEAT, HID), BF16),
            jax.ShapeDtypeStruct((HID, FEAT), BF16),
        ),
        in_specs=[pl.BlockSpec(memory_space=pltpu.HBM)] * 4,
        out_specs=(vmem, vmem, anywhere, anywhere),
        scratch_shapes=[
            pltpu.VMEM((NYL, HALF, FEAT), BF16),
            pltpu.VMEM((NYL, HALF, FEAT), BF16),
            pltpu.VMEM((HALF, FEAT), BF16),
            pltpu.VMEM((HALF, FEAT), BF16),
            pltpu.VMEM((2, FEAT, HID), BF16),
            pltpu.VMEM((2, HID, FEAT), BF16),
            pltpu.VMEM((HALF, HID), F32),
            pltpu.VMEM((HALF, HID), F32),
            pltpu.VMEM((2, 3, 64, HID), BF16),
            pltpu.VMEM((2, 3, 64, HID), BF16),
            pltpu.VMEM((3, ROWS, HID), BF16),
            pltpu.VMEM((3, ROWS, HID), F32),
            pltpu.VMEM((3, ROWS, HID), BF16),
            pltpu.VMEM((3, ROWS, HID), F32),
            pltpu.VMEM((ROWS, HID), F32),
            pltpu.VMEM((TOKENS, HID), BF16),
            pltpu.VMEM((TOKENS, HID), BF16),
            pltpu.VMEM((2, HALF, FEAT), BF16),
            pltpu.VMEM((2, HALF, FEAT), BF16),
            pltpu.VMEM((HALF, FEAT), F32),
            pltpu.VMEM((HALF, FEAT), F32),
            pltpu.VMEM((2, HALF, FEAT), BF16),
            pltpu.VMEM((2, NZ - 1, ROWS, FEAT), BF16),
            pltpu.VMEM((FEAT, HID), BF16),
            pltpu.VMEM((HID, FEAT), BF16),
            pltpu.SemaphoreType.DMA((N_SEM,)),
            pltpu.SemaphoreType.DMA((N_SEM,)),
            pltpu.SemaphoreType.DMA((8,)),
        ],
        compiler_params=pltpu.CompilerParams(
            collective_id=0, has_side_effects=True, vmem_limit_bytes=60 * 1024 * 1024
        ),
    )(tokens, up_weight, down_weight, out_grad)


def solution(mesh):
    return jax.shard_map(
        body,
        mesh=mesh,
        in_specs=(P("tp", "fsdp"), P("fsdp", "tp"), P("tp", "fsdp"), P("tp", "fsdp")),
        out_specs=(P("tp", "fsdp"), P("tp", "fsdp"), P("fsdp", "tp"), P("tp", "fsdp")),
        check_vma=False,
    )
```

```python
import functools
import math

import jax
import jax.numpy as jnp
from jax import lax
from jax.experimental import pallas as pl
from jax.experimental.pallas import tpu as pltpu
from jax.sharding import PartitionSpec as P

MESH = pl.DeviceIdType.MESH
BF16 = jnp.bfloat16
F32 = jnp.float32

NX, NYH, NYL, NZ = 4, 4, 2, 16
ROWS = 16
HALF = NZ * ROWS
TOKENS = NYL * HALF
FEAT, HID = 384, 896
AWAY = (2, 1, -1)
Z_AWAY = (8,) + tuple(s * k for k in range(7, 0, -1) for s in (1, -1))
Z_DIRECT = (8, 6, -6, 3, -3, 1, -1)
FIRST = 7
N_SEM = 208
ORDER = "FBFBFFBFBFBFBFFBFBFBBBGGFB"
GELU_A = math.sqrt(2.0 / math.pi)
GELU_B = 0.044715


def gelu(v):
    return 0.5 * v * (1.0 + jnp.tanh(GELU_A * (v + GELU_B * v * v * v)))


def gelu_slope(v):
    t = jnp.tanh(GELU_A * (v + GELU_B * v * v * v))
    return 0.5 * (1.0 + t) + 0.5 * v * (1.0 - t * t) * GELU_A * (1.0 + 3.0 * GELU_B * v * v)


def dot(a, b, ca=1, cb=0):
    return lax.dot_general(a, b, (((ca,), (cb,)), ((), ())), preferred_element_type=F32)


def kernel(
    tok, up, down, cot, out, in_grad, up_grad, down_grad,
    t0, t1, s0, s1, wu, wd, p0, p1, sx, rx, sy0, sy1, ry0, ry1, pre_ref, h0, h1,
    ob, rb, sum0, sum1, zs, rz, du, dd, send_sem, recv_sem, local_sem,
):
    f = lax.axis_index("fsdp")
    t = lax.axis_index("tp")
    c = lax.rem(f, 2)
    x = lax.rem(f // 2, NX)
    yh = f // (2 * NX)
    yl = t // NZ
    z = lax.rem(t, NZ)

    def dev(x_=None, yh_=None, c_=None, yl_=None, z_=None):
        x_ = x if x_ is None else x_
        yh_ = yh if yh_ is None else yh_
        c_ = c if c_ is None else c_
        yl_ = yl if yl_ is None else yl_
        z_ = z if z_ is None else z_
        return ((yh_ * NX + x_) * 2 + c_, yl_ * NZ + z_)

    def mod(v, n):
        return lax.rem(v + n, n)

    sibling, partner = dev(c_=1 - c), dev(yl_=1 - yl)
    x_peers = [mod(x + k, NX) for k in AWAY]
    y_peers = [mod(yh + k, NYH) for k in AWAY]
    x_devs = [dev(x_=v) for v in x_peers]
    y_devs = [dev(yh_=v) for v in y_peers]

    def z_dev(k):
        return dev(z_=mod(z + k, NZ))

    z_devs = [z_dev(k) for k in Z_AWAY]

    pending = []
    used = [0, 0]

    def local(src, dst):
        copy = pltpu.make_async_copy(src, dst, local_sem.at[used[1]])
        used[1] += 1
        copy.start()
        return copy

    def send(src, dst, to):
        copy = pltpu.make_async_remote_copy(
            src_ref=src, dst_ref=dst, send_sem=send_sem.at[used[0]], recv_sem=recv_sem.at[used[0]],
            device_id=to, device_id_type=MESH,
        )
        used[0] += 1
        copy.start()
        pending.append(copy)
        return copy

    def zrows(k):
        return pl.ds(pl.multiple_of(mod(z + k, NZ) * ROWS, ROWS), ROWS)

    weights = [local(up, wu.at[0]), local(down, wd.at[0])]
    own_rows = [
        local(src, buf.at[yl, zrows(0), :]) for src, buf in ((tok, t0), (cot, t1))
    ]

    barrier = pltpu.get_barrier_semaphore()
    peers = (*z_devs, *y_devs, *x_devs, partner, sibling)
    for peer in peers:
        pl.semaphore_signal(barrier, inc=1, device_id=peer, device_id_type=MESH)
    pl.semaphore_wait(barrier, len(peers))

    done = set()
    weight_copies = []

    def chain(a):
        src, rows_all, rows_sib, part, h, total, result = (
            (tok, t0, s0, p0, h0, sum0, out), (cot, t1, s1, p1, h1, sum1, in_grad)
        )[a]

        mine = rows_all.at[yl, zrows(0), :]
        direct = {k: send(src, mine, z_dev(k)) for k in Z_DIRECT}
        over_y = [send(src, mine, partner)]
        if a == 0:
            weight_copies.extend((send(up, wu.at[1], sibling), send(down, wd.at[1], sibling)))
        yield

        def cross(k):
            there = rows_all.at[yl, zrows(-k), :]
            over_y.append(send(there, there, partner))

        passed = {}
        for k in (1, -1, 3, -3, 6, -6):
            direct[k].wait_recv()
            if abs(k) > 1:
                there = rows_all.at[yl, zrows(-k), :]
                for s in (1, -1):
                    passed[k + s] = send(there, there, z_dev(s))
            cross(k)
        yield
        direct[8].wait_recv()
        cross(8)
        for k, copy in passed.items():
            copy.wait_recv()
            cross(k)
        own_rows[a].wait()
        yield
        for copy in over_y:
            copy.wait_recv()
        across = send(rows_all.at[1 - c], rows_sib, sibling)
        done.add(("rows", a))

        w, contract = ((wu, 0), (wd, 1))[a]
        weights[a].wait()
        part[...] = dot(rows_all[c], w[0], 1, contract)
        weight_copies[a].wait_recv()
        across.wait_recv()
        part[...] += dot(rows_sib[...], w[1], 1, contract)

        def xrows(x_):
            return pl.ds(pl.multiple_of(x_ * 64, 64), 64)

        for i, there in enumerate(x_peers):
            sx[a, i] = part[xrows(there), :].astype(BF16)
        over_x = []
        for there in y_peers + [yh]:
            rows = pl.ds(pl.multiple_of(there * ROWS, ROWS), ROWS)
            over_x.append(
                [send(sx.at[a, i, rows, :], rx.at[a, i, rows, :], to) for i, to in enumerate(x_devs)]
            )
        yield

        def yrows(y_):
            return pl.ds(pl.multiple_of(x * 64 + y_ * ROWS, ROWS), ROWS)

        def sum_x(j, there):
            for copy in over_x[j]:
                copy.wait_recv()
            rows = pl.ds(pl.multiple_of(there * ROWS, ROWS), ROWS)
            got = rx[a, :, rows, :].astype(F32)
            return part[yrows(there), :] + (got[0] + got[1] + got[2])

        copies = []
        for i, (there, to) in enumerate(zip(y_peers, y_devs)):
            value = sum_x(i, there)
            if a == 0:
                sy0[i] = value.astype(BF16)
                copies.append(send(sy0.at[i], ry0.at[i], to))
            else:
                sy1[i] = value
                copies.append(send(sy1.at[i], ry1.at[i], to))
        yield
        value = sum_x(3, yh)
        for copy in copies:
            copy.wait_recv()
        got = ry0[...].astype(F32) if a == 0 else ry1[...]
        value = value + (got[0] + got[1] + got[2])

        def hrows(x_, y_):
            return pl.ds(pl.multiple_of(c * HALF + x_ * 64 + y_ * ROWS, ROWS), ROWS)

        if a == 0:
            pre_ref[...] = value
            h[hrows(x, yh), :] = gelu(value).astype(BF16)
            done.add("pre")
        else:
            assert "pre" in done
            h[hrows(x, yh), :] = (value * gelu_slope(pre_ref[...])).astype(BF16)

        def block(y_, to):
            ref = h.at[hrows(x, y_), :]
            return send(ref, ref, to)

        def column(x_):
            rows = pl.ds(pl.multiple_of(c * HALF + x_ * 64, 64), 64)
            return send(h.at[rows, :], h.at[rows, :], sibling)

        over_yh = [block(yh, to) for to in y_devs]
        over_x = [[block(yh, to)] for to in x_devs]
        yield
        for i in (1, 2, 0):
            over_yh[i].wait_recv()
            for copies, to in zip(over_x, x_devs):
                copies.append(block(mod(yh - AWAY[i], NYH), to))
        columns = [column(x)]
        yield
        for i in (1, 2, 0):
            for copy in over_x[i]:
                copy.wait_recv()
            columns.append(column(mod(x - AWAY[i], NX)))
        yield
        for copy in columns:
            copy.wait_recv()
        done.add(("hidden", a))

        back, contract = ((wd, 0), (wu, 1))[a]

        def product(half):
            rows = h[pl.ds(pl.multiple_of(half * HALF, HALF), HALF), :]
            return dot(rows, back[0], 1, contract)

        ob[a] = product(1 - yl).astype(BF16)
        across = [
            send(ob.at[a, zrows(k), :], rb.at[a, zrows(k), :], partner) for k in Z_AWAY + (0,)
        ]
        total[...] = product(yl)
        yield

        copies = []
        for i, (k, to) in enumerate(zip(Z_AWAY, z_devs)):
            if i == FIRST:
                yield
            across[i].wait_recv()
            zs[a, zrows(k), :] = (total[zrows(k), :] + rb[a, zrows(k), :].astype(F32)).astype(BF16)
            copies.append(send(zs.at[a, zrows(k), :], rz.at[a, i], to))
        across[-1].wait_recv()
        yield
        value = total[zrows(0), :] + rb[a, zrows(0), :].astype(F32)
        for i, copy in reversed(tuple(enumerate(copies))):
            copy.wait_recv()
            value = value + rz[a, i].astype(F32)
        result[...] = value.astype(BF16)

    scale = 1.0 / math.sqrt(TOKENS)
    grads = []

    def down_product():
        dd[...] = (dot(h0[...], t1[...].reshape(TOKENS, FEAT), 0, 0) * scale).astype(BF16)
        grads.append(local(dd, down_grad))

    def up_product():
        du[...] = (dot(t0[...].reshape(TOKENS, FEAT), h1[...], 0, 0) * scale).astype(BF16)
        grads.append(local(du, up_grad))

    steps = {
        "F": chain(0), "B": chain(1), "G": iter((down_product, up_product)),
    }
    for name in ORDER:
        step = next(steps[name], None)
        if step is not None:
            step()
    assert next(steps["F"], "end") == next(steps["B"], "end") == next(steps["G"], "end") == "end"

    for copy in pending:
        copy.wait_send()
    for copy in grads:
        copy.wait()


def body(tokens, up_weight, down_weight, out_grad):
    anywhere = pl.BlockSpec(memory_space=pl.ANY)
    vmem = pl.BlockSpec(memory_space=pltpu.VMEM)
    return pl.pallas_call(
        kernel,
        out_shape=(
            jax.ShapeDtypeStruct((ROWS, FEAT), BF16),
            jax.ShapeDtypeStruct((ROWS, FEAT), BF16),
            jax.ShapeDtypeStruct((FEAT, HID), BF16),
            jax.ShapeDtypeStruct((HID, FEAT), BF16),
        ),
        in_specs=[pl.BlockSpec(memory_space=pltpu.HBM)] * 4,
        out_specs=(vmem, vmem, anywhere, anywhere),
        scratch_shapes=[
            pltpu.VMEM((NYL, HALF, FEAT), BF16),
            pltpu.VMEM((NYL, HALF, FEAT), BF16),
            pltpu.VMEM((HALF, FEAT), BF16),
            pltpu.VMEM((HALF, FEAT), BF16),
            pltpu.VMEM((2, FEAT, HID), BF16),
            pltpu.VMEM((2, HID, FEAT), BF16),
            pltpu.VMEM((HALF, HID), F32),
            pltpu.VMEM((HALF, HID), F32),
            pltpu.VMEM((2, 3, 64, HID), BF16),
            pltpu.VMEM((2, 3, 64, HID), BF16),
            pltpu.VMEM((3, ROWS, HID), BF16),
            pltpu.VMEM((3, ROWS, HID), F32),
            pltpu.VMEM((3, ROWS, HID), BF16),
            pltpu.VMEM((3, ROWS, HID), F32),
            pltpu.VMEM((ROWS, HID), F32),
            pltpu.VMEM((TOKENS, HID), BF16),
            pltpu.VMEM((TOKENS, HID), BF16),
            pltpu.VMEM((2, HALF, FEAT), BF16),
            pltpu.VMEM((2, HALF, FEAT), BF16),
            pltpu.VMEM((HALF, FEAT), F32),
            pltpu.VMEM((HALF, FEAT), F32),
            pltpu.VMEM((2, HALF, FEAT), BF16),
            pltpu.VMEM((2, NZ - 1, ROWS, FEAT), BF16),
            pltpu.VMEM((FEAT, HID), BF16),
            pltpu.VMEM((HID, FEAT), BF16),
            pltpu.SemaphoreType.DMA((N_SEM,)),
            pltpu.SemaphoreType.DMA((N_SEM,)),
            pltpu.SemaphoreType.DMA((8,)),
        ],
        compiler_params=pltpu.CompilerParams(
            collective_id=0, has_side_effects=True, vmem_limit_bytes=52 * 1024 * 1024
        ),
    )(tokens, up_weight, down_weight, out_grad)


def solution(mesh):
    return jax.shard_map(
        body,
        mesh=mesh,
        in_specs=(P("tp", "fsdp"), P("fsdp", "tp"), P("tp", "fsdp"), P("tp", "fsdp")),
        out_specs=(P("tp", "fsdp"), P("tp", "fsdp"), P("fsdp", "tp"), P("tp", "fsdp")),
        check_vma=False,
    )
```
